32 devices in a mesh: groups: 2 (over x), pool: 2 (over core), tp: 8 (over z, y).
Axes of the slice: x: 2, y: 2, z: 4, core: 2. Of those that a mesh axis runs over, the one named last changes fastest.
Arguments:
- hidden_states: bfloat16 [4, 16, 16384], P(None, 'groups', ('pool', 'tp')), parts along dimension 1, may hold values from -6 to 6
- w_query: bfloat16 [16384, 8192], P(('pool', 'tp')), may hold values from -0.046875 to 0.046875
- w_key_value: bfloat16 [16384, 1024], P(('pool', 'tp')), may hold values from -0.046875 to 0.046875
- kv_pages: bfloat16 [96, 128, 1024], P(('groups', 'pool', 'tp')), parts along dimension 0, as said below
- row_pages: int32 [16], P('groups'), parts along dimension 0, may hold values from 1 to 12, 48 in all
- last_pad: int32 [16], P('groups'), parts along dimension 0, may hold values from 0 to 127
- page_dest: int32 [96], P('groups'), parts along dimension 0, may hold values from 0 to 15, as said below
- page_slot: int32 [96], P('groups'), parts along dimension 0, may hold values from 0 to 3, as said below
Outputs:
- attn_out: bfloat16 [4, 16, 8192], P(None, 'groups', ('pool', 'tp')), parts along dimension 1
- decode_cache: bfloat16 [128, 128, 1024], P(('groups', 'pool', 'tp')), parts along dimension 0
The draws below stay inside these ranges and needn't reach their ends.
There are 2 independent parts, one for each index of `groups`. The reference program is written for one: setup_inputs(seed, part) draws one part's arguments, and reference() takes and returns one part's arrays. A program takes and returns all parts, laid end to end along the dimension named above; an argument that names none is the same for every part. Nothing has to cross between parts.
Inputs may be any that keep to these rules, and one draw needn't show every extreme that they name: `kv_pages`: keys in the first 512 columns already carry rotary positions; values follow. `page_dest`: A page written on a device of pool index p goes to a device of pool index 1 - p; the 3 pages written on one device go to 3 different devices; each device receives at most 4 pages, and at least a quarter of the devices of each pool index receive exactly that many. Devices are numbered pool index times 8 plus tp index. `page_slot`: no two pages share a device and a slot. `row_pages`: they sum to 48; the longest request has exactly 12 pages.
All inputs are finite; a program needn't handle non-finite values.
Results may differ from the reference program's by a relative error of at most 0.012.
Values may be sent and summed in bfloat16 or wider, within the bound.
A program may use at most 128 MiB of HBM per device.

```python
import math
import jax
import jax.numpy as jnp
import numpy as np
from jax import lax

D = 16384
QH = 64
KVH = 4
HD = 128
PAGE = 128
STEPS = 4
ROWS = 8
PAGES_DEV = 3
SLOTS_DEV = 4
TOTAL_PAGES = 48
MOST_PAGES = 12
N_POOL = 2
N_TP = 8


def side_targets(key, side):
    count_a = N_TP // 4
    count_b = N_TP - count_a
    reach_a = N_TP // 8
    reach_b = PAGES_DEV - reach_a
    rank_key, label_key = jax.random.split(jax.random.fold_in(key, 11 + side))
    ranking = jax.random.permutation(rank_key, N_TP)
    labels = jax.random.permutation(label_key, N_TP)
    first = ranking[(labels[:, None] + jnp.arange(reach_a)[None, :]) % count_a]
    second = ranking[count_a + (labels[:, None] + jnp.arange(reach_b)[None, :]) % count_b]
    return jnp.concatenate([first, second], axis=1) + (1 - side) * N_TP


def route_pages(key):
    device_count = N_POOL * N_TP
    order_key, offset_key = jax.random.split(jax.random.fold_in(key, 5))
    targets = jnp.concatenate([side_targets(key, 0), side_targets(key, 1)], axis=0)
    order_bits = jax.random.randint(order_key, (device_count, PAGES_DEV), 0, 1 << 20) * PAGES_DEV + jnp.arange(PAGES_DEV)
    ordering = jnp.argsort(order_bits, axis=1)
    targets = jnp.take_along_axis(targets, ordering, axis=1)
    page_dest = targets.reshape(-1).astype(jnp.int32)
    page_ids = jnp.arange(page_dest.shape[0])
    earlier = (page_dest[:, None] == page_dest[None, :]) & (page_ids[:, None] > page_ids[None, :])
    arrival = jnp.sum(earlier.astype(jnp.int32), axis=1)
    offsets = jax.random.randint(offset_key, (device_count,), 0, SLOTS_DEV)
    page_slot = ((arrival + offsets[page_dest]) % SLOTS_DEV).astype(jnp.int32)
    return (page_dest, page_slot)


def draw_page_dest(key, part):
    routes = route_pages(key)
    return routes[0]


def draw_page_slot(key, part):
    routes = route_pages(key)
    return routes[1]


def draw_kv_pages(key, part):
    key = jax.random.fold_in(key, 7)
    value_key = jax.random.fold_in(key, 0)
    shape_all = (PAGES_DEV * N_POOL * N_TP, PAGE, 2 * KVH * HD)
    entries = jax.random.normal(value_key, shape_all, jnp.float32)
    return entries.astype(jnp.bfloat16)


def plant(drawn, stream_key, low, top_value):
    longest = drawn.shape.index(max(drawn.shape))
    spots = []
    for shift in (0, 1):
        where = [jax.random.randint(jax.random.fold_in(stream_key, axis), (), 0, length) for axis, length in enumerate(drawn.shape)]
        where[longest] = (where[longest] + shift) % drawn.shape[longest]
        spots.append(tuple(where))
    return drawn.at[spots[0]].set(low).at[spots[1]].set(top_value)


def block_scale(own_key, dims, cuts, low, high):
    factor_of, own = 1.0, jax.random.fold_in(own_key, 6)
    for position, blocks in cuts:
        steps = jnp.exp(jax.random.uniform(jax.random.fold_in(own, position), (blocks,), jnp.float32, low / len(cuts), high / len(cuts)))
        factor_of = factor_of * jnp.repeat(steps, dims[position] // blocks).reshape([-1 if axis == position else 1 for axis in range(len(dims))])
    return factor_of


def profile(number_of, total, most, lean):
    loads = [(1 << 20) // math.isqrt(grade ** lean) + 1 for grade in range(2, number_of + 1)]
    spare, holding = total - most - (number_of - 1), [1] * (number_of - 1)
    while spare > 0:
        candidates = [i for i in range(number_of - 1) if holding[i] < most]
        mass, remaining = sum([loads[i] for i in candidates]), spare
        for i in candidates:
            more = min(most - holding[i], max(1, remaining * loads[i] // mass), spare)
            holding[i] = holding[i] + more
            spare = spare - more
    return np.array([most] + holding)


def ragged_sizes(key, amount, total, limit, lean):
    if amount == 2:
        one = jax.random.randint(key, (), max(1, total - limit), min(limit, total - 1) + 1)
        return jnp.stack([one, total - one])
    tallies = jnp.asarray(profile(amount, total, limit, lean), jnp.int32)
    couples = (amount - 1) // 2
    giver, sink = tallies[1:1 + 2 * couples:2], tallies[2:2 + 2 * couples:2]
    slack = jnp.minimum(giver - 1, limit - sink)
    shifted = jax.random.randint(jax.random.fold_in(key, 1), (couples,), 0, 1 << 20) % (slack + 1)
    tallies = tallies.at[1:1 + 2 * couples:2].set(giver - shifted).at[2:2 + 2 * couples:2].set(sink + shifted)
    return tallies[jax.random.permutation(jax.random.fold_in(key, 2), amount)]


def scatter_about(own_key, extent, width, limit, cuts=(), kind=jnp.bfloat16):
    result = width * jax.random.normal(own_key, extent, jnp.float32)
    if cuts:
        result = result * block_scale(own_key, extent, cuts, -0.22, 0.18)
    return jnp.clip(result, -limit, limit).astype(kind)


def setup_inputs(seed: int = 0, part: int = 0) -> dict:
    seeds = jax.random.split(jax.random.key(seed), 9)
    part_splits = jax.random.split(jax.random.fold_in(seeds[8], part), 9)
    return {
        "hidden_states": scatter_about(part_splits[0], (STEPS, ROWS, D), 1.0, 6.0, ((2, 16),)),
        "w_query": scatter_about(seeds[1], (D, QH * HD), D ** -0.5, 0.046875, ((0, 16),)),
        "w_key_value": scatter_about(seeds[2], (D, 2 * KVH * HD), D ** -0.5, 0.046875, ((0, 16),)),
        "kv_pages": draw_kv_pages(jax.random.fold_in(jax.random.fold_in(seeds[8], part), 71), part),
        "row_pages": ragged_sizes(part_splits[4], ROWS, TOTAL_PAGES, MOST_PAGES, 2).astype(jnp.int32),
        "last_pad": plant(jax.random.randint(part_splits[5], (ROWS,), 0, PAGE), jax.random.fold_in(part_splits[5], 1), 0, PAGE - 1).astype(jnp.int32),
        "page_dest": draw_page_dest(jax.random.fold_in(jax.random.fold_in(seeds[8], part), 71), part),
        "page_slot": draw_page_slot(jax.random.fold_in(jax.random.fold_in(seeds[8], part), 71), part),
    }


def rotate(vectors, positions):
    half_size = vectors.shape[-1] // 2
    frequency = 500000.0 ** (-jnp.arange(half_size, dtype=jnp.float32) * 2.0 / vectors.shape[-1])
    angles = positions[:, :, None, None] * frequency
    cosine = jnp.cos(angles)
    sine_part = jnp.sin(angles)
    first_half = vectors[..., :half_size]
    second_half = vectors[..., half_size:]
    return jnp.concatenate([first_half * cosine - second_half * sine_part, second_half * cosine + first_half * sine_part], axis=-1)

def page_meta(row_pages, last_pad, total_pages):
    page_ids = jnp.arange(total_pages, dtype=jnp.int32)
    row_ends = jnp.cumsum(row_pages).astype(jnp.int32)
    page_row = lax.optimization_barrier(jnp.sum((page_ids[:, None] >= row_ends[None, :]).astype(jnp.int32), axis=1))
    last_hit = (page_ids[:, None] == row_ends[None, :] - 1).astype(jnp.int32)
    page_valid = PAGE - lax.optimization_barrier(jnp.sum(last_hit * last_pad[None, :], axis=1))
    return (page_row, page_valid)

def reference(hidden_states, w_query, w_key_value, kv_pages, row_pages, last_pad, page_dest, page_slot):
    step_count, row_count, model_width = hidden_states.shape
    group_size = QH // KVH
    score_scale = 1.0 / math.sqrt(HD)
    flat_rows = hidden_states.reshape(step_count * row_count, model_width)
    query_sum = jnp.dot(flat_rows, w_query, preferred_element_type=jnp.float32)
    kv_sum = jnp.dot(flat_rows, w_key_value, preferred_element_type=jnp.float32)
    positions = (row_pages * PAGE - last_pad)[None, :] + jnp.arange(step_count, dtype=jnp.int32)[:, None]
    positions = positions.astype(jnp.float32)
    queries = rotate(query_sum.reshape(step_count, row_count, QH, HD), positions).astype(jnp.bfloat16)
    kv_heads = kv_sum.reshape(step_count, row_count, 2, KVH, HD)
    new_keys = rotate(kv_heads[:, :, 0], positions).astype(jnp.bfloat16)
    new_values = kv_heads[:, :, 1].astype(jnp.bfloat16)
    total_pages = kv_pages.shape[0]
    page_len = kv_pages.shape[1]
    page_row, page_valid = page_meta(row_pages, last_pad, total_pages)
    keys_all = kv_pages[:, :, :KVH * HD].astype(jnp.float32).reshape(total_pages * page_len, KVH, HD)
    values_all = kv_pages[:, :, KVH * HD:].astype(jnp.float32).reshape(total_pages * page_len, KVH, HD)
    token_row = jnp.repeat(page_row, page_len)
    token_live = (jnp.arange(page_len, dtype=jnp.int32)[None, :] < page_valid[:, None]).reshape(-1)
    causal = jnp.arange(step_count)[None, :] <= jnp.arange(step_count)[:, None]

    def one_row(row_index):
        query_row = queries[:, row_index].astype(jnp.float32).reshape(step_count, KVH, group_size, HD)
        scores = jnp.einsum('tcgh,pch->tcgp', query_row, keys_all) * score_scale
        live_tokens = (token_row == row_index) & token_live
        scores = jnp.where(live_tokens[None, None, None, :], scores, -1e+30)
        fresh_scores = jnp.einsum('tcgh,uch->tcgu', query_row, new_keys[:, row_index].astype(jnp.float32)) * score_scale
        fresh_scores = jnp.where(causal[:, None, None, :], fresh_scores, -1e+30)
        row_top = jnp.maximum(lax.optimization_barrier(jnp.max(scores, axis=-1)), lax.optimization_barrier(jnp.max(fresh_scores, axis=-1)))
        weights = jnp.exp(scores - row_top[..., None])
        fresh_weights = jnp.exp(fresh_scores - row_top[..., None])
        total_sum = lax.optimization_barrier(jnp.sum(weights, axis=-1)) + lax.optimization_barrier(jnp.sum(fresh_weights, axis=-1))
        rounded = lax.optimization_barrier(weights.astype(jnp.bfloat16)).astype(jnp.float32)
        fresh_rounded = lax.optimization_barrier(fresh_weights.astype(jnp.bfloat16)).astype(jnp.float32)
        accumulated = jnp.einsum('tcgp,pch->tcgh', rounded, values_all)
        accumulated = accumulated + jnp.einsum('tcgu,uch->tcgh', fresh_rounded, new_values[:, row_index].astype(jnp.float32))
        return (accumulated / total_sum[..., None]).reshape(step_count, QH * HD).astype(jnp.bfloat16)
    attended = lax.map(one_row, jnp.arange(row_count, dtype=jnp.int32))
    attn_out = jnp.transpose(attended, (1, 0, 2))
    slot_total = N_POOL * N_TP * SLOTS_DEV
    decode_cache = jnp.zeros((slot_total, page_len, kv_pages.shape[2]), jnp.bfloat16)
    decode_cache = decode_cache.at[(page_dest * SLOTS_DEV + page_slot).astype(jnp.int32)].set(kv_pages)
    return (attn_out, decode_cache)
```

```python
import functools
import math

import jax
import jax.numpy as jnp
import numpy as np
from jax import lax
from jax.experimental import pallas as pl
from jax.experimental.pallas import tpu as pltpu
from jax.sharding import PartitionSpec as P

QH = 64
KVH = 4
HD = 128
PAGE = 128


MESH = pl.DeviceIdType.MESH
DEAD = -1e30


def dot(a, b, dims, precision=None):
    return lax.dot_general(
        a, b, (dims, ((), ())), preferred_element_type=jnp.float32, precision=precision
    )


def attend(keys, values, queries, mask):
    scores = dot(queries, keys, ((1,), (1,))) * (1.0 / math.sqrt(HD))
    scores = jnp.where(mask, scores, DEAD)
    top = jnp.maximum(jnp.max(scores, axis=1, keepdims=True), 0.5 * DEAD)
    weights = jnp.exp(scores - top)
    total = jnp.sum(weights, axis=1, keepdims=True)
    acc = dot(weights.astype(jnp.bfloat16), values, ((1,), (0,)))
    return top, total, acc


def kernel(
    n, tp_count, steps, slot_count,
    row_pages, last_pad, hidden, w_query, w_kv, pages, page_dest, page_slot, cosine, sine,
    flat_page, flat_base, src_page, src_base, row_page,
    attn, cache,
    wq_v, wkv_v, kv_part, core_s, core_r, keep, y_s, y_r, z_s, z_r, q_mine, q_s, q_r,
    num_s, num_r, stat_s, stat_r, targets, bucket, incoming,
    load_sem, page_send, page_recv, core_send, core_recv, y_send, y_recv, z_send, z_recv,
    ag_send, ag_recv, num_send, num_recv, stat_send, stat_recv,
):
    rows = hidden.shape[0]
    row_count = rows // steps
    page_count, page_len = pages.shape[0], pages.shape[1]
    heads = QH // n
    cols = heads * HD
    owners = n // KVH
    lanes = heads * page_count * steps
    tokens = page_count * page_len
    pool = lax.axis_index("pool")
    tp = lax.axis_index("tp")
    me = pool * tp_count + tp
    z_count = tp_count // 2
    z, y = tp // 2, lax.rem(tp, 2)

    def peer(i):
        return lax.rem(me + i, n)

    def place(d):
        return {"pool": d // tp_count, "tp": lax.rem(d, tp_count)}

    def remote(src, dst, send, recv, where):
        return pltpu.make_async_remote_copy(
            src_ref=src, dst_ref=dst, send_sem=send, recv_sem=recv,
            device_id=where, device_id_type=MESH,
        )

    z_order = list(range(1, z_count)) + [0]
    blocks = [(side, j, rel) for side in (1, 0) for j in z_order for rel in (1, 0)]

    def owner_of(side, j, rel):
        to_pool = 1 - pool if side else pool
        to_y = 1 - y if rel else y
        return to_pool * tp_count + 2 * lax.rem(z + j, z_count) + to_y

    loads = [pltpu.make_async_copy(w_kv, wkv_v, load_sem.at[n])]
    for at, block in enumerate(blocks):
        begin = pl.multiple_of(owner_of(*block) * cols, cols)
        loads.append(
            pltpu.make_async_copy(w_query.at[:, pl.ds(begin, cols)], wq_v.at[at], load_sem.at[at])
        )
    for load in loads:
        load.start()

    barrier = pltpu.get_barrier_semaphore()
    for i in range(1, n):
        pl.semaphore_signal(barrier, inc=1, device_id=place(peer(i)), device_id_type=MESH)

    page_id = lax.broadcasted_iota(jnp.int32, page_dest.shape, 1)
    page_order = [(i + tp_count // 2) % tp_count for i in range(tp_count)]
    page_copies = {}
    for i in page_order:
        to = lax.rem(tp + i, tp_count)
        hit = (page_dest[...] == (1 - pool) * tp_count + to) & (page_id >= me * page_count)
        hit = hit & (page_id < (me + 1) * page_count)
        picked = jnp.max(jnp.where(hit, page_id - me * page_count, 0))
        bucket[i] = pages[picked]
        page_copies[i] = remote(
            bucket.at[i], incoming.at[tp], page_send.at[i], page_recv.at[i],
            {"pool": 1 - pool, "tp": to},
        )
    pl.semaphore_wait(barrier, n - 1)
    for i in page_order[ : 3 * tp_count // 8]:
        page_copies[i].start()

    loads[0].wait()
    kv_part[...] = dot(hidden[...], wkv_v[...], ((1,), (0,)))

    def partial(at, block, write):
        loads[1 + at].wait()
        write(slice(0, cols), dot(hidden[...], wq_v[at], ((1,), (0,))))
        head = owner_of(*block) // owners
        key_at = pl.multiple_of(head * HD, HD)
        value_at = pl.multiple_of((KVH + head) * HD, HD)
        write(slice(cols, cols + HD), kv_part[:, pl.ds(key_at, HD)])
        write(slice(cols + HD, cols + 2 * HD), kv_part[:, pl.ds(value_at, HD)])

    core_copies, y_copies, z_copies = {}, {}, {}
    for at, block in enumerate(blocks):
        side, j, rel = block
        if side:
            def write(span, value, j=j, rel=rel):
                core_s[j, rel, :, span] = value

            partial(at, block, write)
            core_copies[j, rel] = remote(
                core_s.at[j, rel], core_r.at[j, rel], core_send.at[j, rel], core_recv.at[j, rel],
                {"pool": 1 - pool, "tp": tp},
            )
            core_copies[j, rel].start()
            continue
        if rel:
            def write(span, value, j=j):
                y_s[j, :, span] = value + core_r[j, 1, :, span]
        else:
            def write(span, value, j=j):
                keep[j, :, span] = value + core_r[j, 0, :, span]

        core_copies[j, rel].wait_recv()
        partial(at, block, write)
        if rel:
            y_copies[j] = remote(
                y_s.at[j], y_r.at[j], y_send.at[j], y_recv.at[j],
                {"pool": pool, "tp": 2 * z + 1 - y},
            )
            y_copies[j].start()
    for i in page_order[3 * tp_count // 8 : 4 * tp_count // 8]:
        page_copies[i].start()
    for j in z_order:
        y_copies[j].wait_recv()
        if j:
            z_s[j] = (keep[j] + y_r[j]).astype(z_s.dtype)
            z_copies[j] = remote(
                z_s.at[j], z_r.at[j], z_send.at[j], z_recv.at[j],
                {"pool": pool, "tp": 2 * lax.rem(z + j, z_count) + y},
            )
            z_copies[j].start()
    total = keep[0] + y_r[0]

    def target(page, base):
        value = base
        end = jnp.int32(0)
        for r in range(row_count - 1):
            end = end + row_pages[r]
            value = value + (page >= end).astype(jnp.int32)
        return value

    targets[...] = target(src_page[...], src_base[...])
    flat = target(flat_page[...], flat_base[...])
    pick = lax.broadcasted_iota(jnp.int32, (heads * rows, n * lanes), 0) == flat
    pick = pick.astype(jnp.float32).astype(jnp.bfloat16)
    token = lax.broadcasted_iota(jnp.int32, (1, tokens), 1)
    token_page = token // page_len
    valid = jnp.full((1, tokens), page_len, jnp.int32)
    end = jnp.int32(0)
    for r in range(row_count):
        end = end + row_pages[r]
        valid = valid - jnp.where(token_page + me * page_count == end - 1, last_pad[r], 0)
    mask = (token % page_len < valid) & (token_page == row_page[...])

    for j in z_order[:-1]:
        z_copies[j].wait_recv()
        total += z_r[j].astype(jnp.float32)

    def rotated(x):
        return (x * cosine[...] + pltpu.roll(x, HD // 2, 1) * sine[...]).astype(jnp.bfloat16)

    for h in range(heads):
        q_mine[h * rows : (h + 1) * rows, :] = rotated(total[:, h * HD : (h + 1) * HD])
    q_s[...] = dot(pick, q_mine[...], ((0,), (0,))).astype(jnp.bfloat16).reshape(n, lanes, HD)
    ag_copies = []
    for i in range(1, n):
        d = peer(i)
        copy = remote(q_s.at[d], q_r.at[me], ag_send.at[i], ag_recv.at[i], place(d))
        copy.start()
        ag_copies.append(copy)
    for i in page_order[4 * tp_count // 8 : ]:
        page_copies[i].start()
    q_r[me] = q_s[me]

    new_key = rotated(total[:, cols : cols + HD])
    new_value = total[:, cols + HD :].astype(jnp.bfloat16)
    key_id = lax.broadcasted_iota(jnp.int32, (heads * rows, rows), 1)
    query_id = lax.broadcasted_iota(jnp.int32, (heads * rows, rows), 0) % rows
    fresh_mask = (key_id % row_count == query_id % row_count) & (
        key_id // row_count <= query_id // row_count
    )
    fresh_top, fresh_total, fresh_acc = attend(new_key, new_value, q_mine[...], fresh_mask)

    for copy in ag_copies:
        copy.wait_recv()
    width = owners * lanes
    stat_lane = lax.broadcasted_iota(jnp.int32, (width, HD), 1)
    for c in range(KVH):
        queries = q_r[c * owners : (c + 1) * owners].reshape(width, HD)
        keys = pages[:, :, c * HD : (c + 1) * HD].reshape(tokens, HD)
        values = pages[:, :, (KVH + c) * HD : (KVH + c + 1) * HD].reshape(tokens, HD)
        top, weight, acc = attend(keys, values, queries, mask)
        num_s[c * owners : (c + 1) * owners] = acc.astype(num_s.dtype).reshape(owners, lanes, HD)
        stats = jnp.transpose(jnp.where(stat_lane == 0, top, weight))
        for o in range(owners):
            stat_s[c * owners + o] = stats[:8, o * lanes : (o + 1) * lanes]
    last_copies = []
    for i in range(1, n):
        d = peer(i)
        copies = (
            remote(stat_s.at[d], stat_r.at[i], stat_send.at[i], stat_recv.at[i], place(d)),
            remote(num_s.at[d], num_r.at[i], num_send.at[i], num_recv.at[i], place(d)),
        )
        for copy in copies:
            copy.start()
        last_copies.append(copies)

    stat_r[0] = stat_s[me]
    num_r[0] = num_s[me]
    query = lax.broadcasted_iota(jnp.int32, (heads * rows, lanes), 0)
    top = fresh_top
    for i in range(n):
        if i:
            last_copies[i - 1][0].wait_recv()
        hit = query == targets[pl.ds(lax.rem(me - i + n, n), 1), :]
        best = jnp.where(hit, stat_r[i, 0:1, :], DEAD)
        top = jnp.maximum(top, jnp.max(best, axis=1, keepdims=True))
    scale = jnp.exp(fresh_top - top)
    weight = fresh_total * scale
    acc = fresh_acc * scale
    for i in range(n):
        hit = query == targets[pl.ds(lax.rem(me - i + n, n), 1), :]
        scales = jnp.exp(jnp.where(hit, stat_r[i, 0:1, :], 2 * DEAD) - top)
        weight += jnp.sum(jnp.where(hit, scales * stat_r[i, 1:2, :], 0.0), axis=1, keepdims=True)
        if i:
            last_copies[i - 1][1].wait_recv()
        acc += dot(
            jnp.where(hit, scales, 0.0), num_r[i].astype(jnp.float32), ((1,), (0,)),
            lax.Precision.HIGHEST,
        )
    out = (acc / weight).astype(jnp.bfloat16)
    for h in range(heads):
        attn[:, h * HD : (h + 1) * HD] = out[h * rows : (h + 1) * rows, :]

    for copy in page_copies.values():
        copy.wait_recv()
    for s in range(slot_count):
        hit = (page_dest[...] == me) & (page_slot[...] == s)
        found = jnp.sum(hit.astype(jnp.int32))
        source = jnp.max(jnp.where(hit, page_id, 0)) // page_count
        source = lax.rem(source, tp_count)
        cache[s] = jnp.where(found > 0, incoming[source], jnp.zeros_like(incoming[0]))
    for group in (core_copies, y_copies, z_copies, page_copies):
        for copy in group.values():
            copy.wait_send()
    for copy in ag_copies + [c for pair in last_copies for c in pair]:
        copy.wait_send()


def on_device(
    hidden_states, w_query, w_key_value, kv_pages, row_pages, last_pad, page_dest, page_slot
):
    steps, row_count, width_part = hidden_states.shape
    n = lax.axis_size(("pool", "tp"))
    tp_count = lax.axis_size("tp")
    z_count = tp_count // 2
    slot_count = tp_count // 2
    rows = steps * row_count
    flat_rows = hidden_states.reshape(rows, width_part)
    positions = (row_pages * PAGE - last_pad)[None, :] + jnp.arange(steps, dtype=jnp.int32)[:, None]
    half_size = HD // 2
    frequency = 500000.0 ** (-jnp.arange(half_size, dtype=jnp.float32) * 2.0 / HD)
    frequency = jnp.concatenate([frequency, frequency])
    angles = positions.astype(jnp.float32).reshape(rows, 1) * frequency
    cosine = jnp.cos(angles)
    sine = jnp.sin(angles) * jnp.where(jnp.arange(HD) < half_size, -1.0, 1.0)
    page_count, page_len, page_width = kv_pages.shape

    heads = QH // n
    cols = heads * HD
    owners = n // KVH
    lanes = heads * page_count * steps
    index = np.arange(n * lanes).reshape(n, heads, page_count, steps)
    source, head, page, step = np.unravel_index(index, index.shape)
    src_page = (source * page_count + page).astype(np.int32).reshape(n, lanes)
    src_base = (head * rows + step * row_count).astype(np.int32).reshape(n, lanes)
    row_page = page[:owners].astype(np.int32).reshape(owners * lanes, 1)

    vmem = pl.BlockSpec(memory_space=pltpu.VMEM)
    smem = pl.BlockSpec(memory_space=pltpu.SMEM)
    hbm = pl.BlockSpec(memory_space=pl.ANY)
    dma = pltpu.SemaphoreType.DMA
    block = (rows, cols + 2 * HD)
    f32, bf16 = jnp.float32, jnp.bfloat16
    attn, decode_cache = pl.pallas_call(
        functools.partial(kernel, n, tp_count, steps, slot_count),
        out_shape=(
            jax.ShapeDtypeStruct((rows, cols), bf16),
            jax.ShapeDtypeStruct((slot_count, page_len, page_width), bf16),
        ),
        in_specs=[smem, smem, vmem, hbm, hbm] + [vmem] * 10,
        out_specs=(vmem, vmem),
        scratch_shapes=[
            pltpu.VMEM((n, width_part, cols), bf16),
            pltpu.VMEM(w_key_value.shape, bf16),
            pltpu.VMEM((rows, w_key_value.shape[1]), f32),
            pltpu.VMEM((z_count, 2) + block, f32),
            pltpu.VMEM((z_count, 2) + block, f32),
            pltpu.VMEM((z_count,) + block, f32),
            pltpu.VMEM((z_count,) + block, f32),
            pltpu.VMEM((z_count,) + block, f32),
            pltpu.VMEM((z_count,) + block, jnp.float32),
            pltpu.VMEM((z_count,) + block, jnp.float32),
            pltpu.VMEM((heads * rows, HD), bf16),
            pltpu.VMEM((n, lanes, HD), bf16),
            pltpu.VMEM((n, lanes, HD), bf16),
            pltpu.VMEM((n, lanes, HD), jnp.float32),
            pltpu.VMEM((n, lanes, HD), jnp.float32),
            pltpu.VMEM((n, 8, lanes), f32),
            pltpu.VMEM((n, 8, lanes), f32),
            pltpu.VMEM((n, lanes), jnp.int32),
            pltpu.VMEM((tp_count, page_len, page_width), bf16),
            pltpu.VMEM((tp_count, page_len, page_width), bf16),
            dma((n + 1,)),
            dma((tp_count,)),
            dma((tp_count,)),
            dma((z_count, 2)),
            dma((z_count, 2)),
        ]
        + [dma((z_count,))] * 4
        + [dma((n,))] * 6,
        compiler_params=pltpu.CompilerParams(
            collective_id=0, has_side_effects=True, vmem_limit_bytes=62 * 1024 * 1024
        ),
    )(
        row_pages, last_pad, flat_rows, w_query, w_key_value, kv_pages,
        page_dest.reshape(1, -1), page_slot.reshape(1, -1), cosine, sine,
        src_page.reshape(1, -1), src_base.reshape(1, -1), src_page, src_base, row_page,
    )
    return (attn.reshape(steps, row_count, cols), decode_cache)


def solution(mesh):
    placed = (
        P(None, "groups", ("pool", "tp")),
        P(("pool", "tp"), None),
        P(("pool", "tp"), None),
        P(("groups", "pool", "tp"), None, None),
        P("groups"),
        P("groups"),
        P("groups"),
        P("groups"),
    )
    return jax.shard_map(
        on_device,
        mesh=mesh,
        in_specs=placed,
        out_specs=(P(None, "groups", ("pool", "tp")), P(("groups", "pool", "tp"), None, None)),
        check_vma=False,
    )
```

```python
import functools
import math

import jax
import jax.numpy as jnp
import numpy as np
from jax import lax
from jax.experimental import pallas as pl
from jax.experimental.pallas import tpu as pltpu
from jax.sharding import PartitionSpec as P

QH = 64
KVH = 4
HD = 128
PAGE = 128


MESH = pl.DeviceIdType.MESH
DEAD = -1e30


def dot(a, b, dims, precision=None):
    return lax.dot_general(
        a, b, (dims, ((), ())), preferred_element_type=jnp.float32, precision=precision
    )


def attend(keys, values, queries, mask):
    scores = dot(queries, keys, ((1,), (1,))) * (1.0 / math.sqrt(HD))
    scores = jnp.where(mask, scores, DEAD)
    top = jnp.maximum(jnp.max(scores, axis=1, keepdims=True), 0.5 * DEAD)
    weights = jnp.exp(scores - top)
    total = jnp.sum(weights, axis=1, keepdims=True)
    acc = dot(weights.astype(jnp.bfloat16), values, ((1,), (0,)))
    return top, total, acc


def kernel(
    n, tp_count, steps, slot_count,
    row_pages, last_pad, hidden, w_query, w_kv, pages, page_dest, page_slot, cosine, sine,
    flat_page, flat_base, src_page, src_base, row_page,
    attn, cache,
    wq_v, wkv_v, kv_part, core_s, core_r, keep, y_s, y_r, w_s, w_r, z_s, z_r, q_mine, q_s, q_r,
    num_s, num_r, stat_s, stat_r, targets, bucket, incoming,
    load_sem, page_send, page_recv, core_send, core_recv, y_send, y_recv, w_send, w_recv, z_send, z_recv,
    ag_send, ag_recv, num_send, num_recv, stat_send, stat_recv,
):
    rows = hidden.shape[0]
    row_count = rows // steps
    page_count, page_len = pages.shape[0], pages.shape[1]
    heads = QH // n
    cols = heads * HD
    owners = n // KVH
    lanes = heads * page_count * steps
    tokens = page_count * page_len
    pool = lax.axis_index("pool")
    tp = lax.axis_index("tp")
    me = pool * tp_count + tp
    z_count = tp_count // 2
    z, y = tp // 2, lax.rem(tp, 2)

    def peer(i):
        return lax.rem(me + i, n)

    def place(d):
        return {"pool": d // tp_count, "tp": lax.rem(d, tp_count)}

    def remote(src, dst, send, recv, where):
        return pltpu.make_async_remote_copy(
            src_ref=src, dst_ref=dst, send_sem=send, recv_sem=recv,
            device_id=where, device_id_type=MESH,
        )

    pairs = z_count // 2
    pair_order = list(range(1, pairs)) + [0]
    z_order = [2 * j + flip for j in pair_order for flip in (1, 0)]
    z_pair, z_low = z // 2, lax.rem(z, 2)
    blocks = [(side, j, rel) for side in (1, 0) for j in z_order for rel in (1, 0)]

    def owner_of(side, j, rel):
        to_pool = 1 - pool if side else pool
        to_y = 1 - y if rel else y
        to_low = 1 - z_low if j % 2 else z_low
        to_z = 2 * lax.rem(z_pair + j // 2, pairs) + to_low
        return to_pool * tp_count + 2 * to_z + to_y

    loads = [pltpu.make_async_copy(w_kv, wkv_v, load_sem.at[n])]
    for at, block in enumerate(blocks):
        begin = pl.multiple_of(owner_of(*block) * cols, cols)
        loads.append(
            pltpu.make_async_copy(w_query.at[:, pl.ds(begin, cols)], wq_v.at[at], load_sem.at[at])
        )
    for load in loads:
        load.start()

    barrier = pltpu.get_barrier_semaphore()
    for i in range(1, n):
        pl.semaphore_signal(barrier, inc=1, device_id=place(peer(i)), device_id_type=MESH)

    page_id = lax.broadcasted_iota(jnp.int32, page_dest.shape, 1)
    page_order = [(i + tp_count // 2) % tp_count for i in range(tp_count)]
    page_copies = {}
    for i in page_order:
        to = lax.rem(tp + i, tp_count)
        hit = (page_dest[...] == (1 - pool) * tp_count + to) & (page_id >= me * page_count)
        hit = hit & (page_id < (me + 1) * page_count)
        picked = jnp.max(jnp.where(hit, page_id - me * page_count, 0))
        bucket[i] = pages[picked]
        page_copies[i] = remote(
            bucket.at[i], incoming.at[tp], page_send.at[i], page_recv.at[i],
            {"pool": 1 - pool, "tp": to},
        )
    pl.semaphore_wait(barrier, n - 1)
    for i in page_order[ : 3 * tp_count // 8]:
        page_copies[i].start()

    loads[0].wait()
    kv_part[...] = dot(hidden[...], wkv_v[...], ((1,), (0,)))

    def partial(at, block, write):
        loads[1 + at].wait()
        write(slice(0, cols), dot(hidden[...], wq_v[at], ((1,), (0,))))
        head = owner_of(*block) // owners
        key_at = pl.multiple_of(head * HD, HD)
        value_at = pl.multiple_of((KVH + head) * HD, HD)
        write(slice(cols, cols + HD), kv_part[:, pl.ds(key_at, HD)])
        write(slice(cols + HD, cols + 2 * HD), kv_part[:, pl.ds(value_at, HD)])

    core_copies, y_copies, z_copies = {}, {}, {}
    for at, block in enumerate(blocks):
        side, j, rel = block
        if side:
            def write(span, value, j=j, rel=rel):
                core_s[j, rel, :, span] = value

            partial(at, block, write)
            core_copies[j, rel] = remote(
                core_s.at[j, rel], core_r.at[j, rel], core_send.at[j, rel], core_recv.at[j, rel],
                {"pool": 1 - pool, "tp": tp},
            )
            core_copies[j, rel].start()
            continue
        if rel:
            def write(span, value, j=j):
                y_s[j, :, span] = value + core_r[j, 1, :, span]
        else:
            def write(span, value, j=j):
                keep[j, :, span] = value + core_r[j, 0, :, span]

        core_copies[j, rel].wait_recv()
        partial(at, block, write)
        if rel:
            y_copies[j] = remote(
                y_s.at[j], y_r.at[j], y_send.at[j], y_recv.at[j],
                {"pool": pool, "tp": 2 * z + 1 - y},
            )
            y_copies[j].start()
    w_copies = {}
    for k in z_order:
        y_copies[k].wait_recv()
        if k % 2:
            j = k // 2
            w_s[j] = keep[k] + y_r[k]
            w_copies[j] = remote(
                w_s.at[j], w_r.at[j], w_send.at[j], w_recv.at[j],
                {"pool": pool, "tp": 2 * (2 * z_pair + 1 - z_low) + y},
            )
            w_copies[j].start()
    for j in pair_order:
        w_copies[j].wait_recv()
        if j:
            z_s[j] = (keep[2 * j] + y_r[2 * j] + w_r[j]).astype(z_s.dtype)
            z_copies[j] = remote(
                z_s.at[j], z_r.at[j], z_send.at[j], z_recv.at[j],
                {"pool": pool, "tp": 2 * (2 * lax.rem(z_pair + j, pairs) + z_low) + y},
            )
            z_copies[j].start()
    total = keep[0] + y_r[0] + w_r[0]

    def target(page, base):
        value = base
        end = jnp.int32(0)
        for r in range(row_count - 1):
            end = end + row_pages[r]
            value = value + (page >= end).astype(jnp.int32)
        return value

    targets[...] = target(src_page[...], src_base[...])
    flat = target(flat_page[...], flat_base[...])
    pick = lax.broadcasted_iota(jnp.int32, (heads * rows, n * lanes), 0) == flat
    pick = pick.astype(jnp.float32).astype(jnp.bfloat16)
    token = lax.broadcasted_iota(jnp.int32, (1, tokens), 1)
    token_page = token // page_len
    valid = jnp.full((1, tokens), page_len, jnp.int32)
    end = jnp.int32(0)
    for r in range(row_count):
        end = end + row_pages[r]
        valid = valid - jnp.where(token_page + me * page_count == end - 1, last_pad[r], 0)
    mask = (token % page_len < valid) & (token_page == row_page[...])

    for j in pair_order[:-1]:
        z_copies[j].wait_recv()
        total += z_r[j].astype(jnp.float32)

    def rotated(x):
        return (x * cosine[...] + pltpu.roll(x, HD // 2, 1) * sine[...]).astype(jnp.bfloat16)

    for h in range(heads):
        q_mine[h * rows : (h + 1) * rows, :] = rotated(total[:, h * HD : (h + 1) * HD])
    q_s[...] = dot(pick, q_mine[...], ((0,), (0,))).astype(jnp.bfloat16).reshape(n, lanes, HD)
    ag_copies = []
    for i in range(1, n):
        d = peer(i)
        copy = remote(q_s.at[d], q_r.at[me], ag_send.at[i], ag_recv.at[i], place(d))
        copy.start()
        ag_copies.append(copy)
    for i in page_order[3 * tp_count // 8 : ]:
        page_copies[i].start()
    q_r[me] = q_s[me]

    new_key = rotated(total[:, cols : cols + HD])
    new_value = total[:, cols + HD :].astype(jnp.bfloat16)
    key_id = lax.broadcasted_iota(jnp.int32, (heads * rows, rows), 1)
    query_id = lax.broadcasted_iota(jnp.int32, (heads * rows, rows), 0) % rows
    fresh_mask = (key_id % row_count == query_id % row_count) & (
        key_id // row_count <= query_id // row_count
    )
    fresh_top, fresh_total, fresh_acc = attend(new_key, new_value, q_mine[...], fresh_mask)

    for copy in ag_copies:
        copy.wait_recv()
    width = owners * lanes
    stat_lane = lax.broadcasted_iota(jnp.int32, (width, HD), 1)
    for c in range(KVH):
        queries = q_r[c * owners : (c + 1) * owners].reshape(width, HD)
        keys = pages[:, :, c * HD : (c + 1) * HD].reshape(tokens, HD)
        values = pages[:, :, (KVH + c) * HD : (KVH + c + 1) * HD].reshape(tokens, HD)
        top, weight, acc = attend(keys, values, queries, mask)
        num_s[c * owners : (c + 1) * owners] = acc.astype(num_s.dtype).reshape(owners, lanes, HD)
        stats = jnp.transpose(jnp.where(stat_lane == 0, top, weight))
        for o in range(owners):
            stat_s[c * owners + o] = stats[:8, o * lanes : (o + 1) * lanes]
    last_copies = []
    for i in range(1, n):
        d = peer(i)
        copies = (
            remote(stat_s.at[d], stat_r.at[i], stat_send.at[i], stat_recv.at[i], place(d)),
            remote(num_s.at[d], num_r.at[i], num_send.at[i], num_recv.at[i], place(d)),
        )
        for copy in copies:
            copy.start()
        last_copies.append(copies)

    stat_r[0] = stat_s[me]
    num_r[0] = num_s[me]
    query = lax.broadcasted_iota(jnp.int32, (heads * rows, lanes), 0)
    top = fresh_top
    for i in range(n):
        if i:
            last_copies[i - 1][0].wait_recv()
        hit = query == targets[pl.ds(lax.rem(me - i + n, n), 1), :]
        best = jnp.where(hit, stat_r[i, 0:1, :], DEAD)
        top = jnp.maximum(top, jnp.max(best, axis=1, keepdims=True))
    scale = jnp.exp(fresh_top - top)
    weight = fresh_total * scale
    acc = fresh_acc * scale
    for i in range(n):
        hit = query == targets[pl.ds(lax.rem(me - i + n, n), 1), :]
        scales = jnp.exp(jnp.where(hit, stat_r[i, 0:1, :], 2 * DEAD) - top)
        weight += jnp.sum(jnp.where(hit, scales * stat_r[i, 1:2, :], 0.0), axis=1, keepdims=True)
        if i:
            last_copies[i - 1][1].wait_recv()
        acc += dot(
            jnp.where(hit, scales, 0.0), num_r[i].astype(jnp.float32), ((1,), (0,)),
            lax.Precision.HIGHEST,
        )
    out = (acc / weight).astype(jnp.bfloat16)
    for h in range(heads):
        attn[:, h * HD : (h + 1) * HD] = out[h * rows : (h + 1) * rows, :]

    for copy in page_copies.values():
        copy.wait_recv()
    for s in range(slot_count):
        hit = (page_dest[...] == me) & (page_slot[...] == s)
        found = jnp.sum(hit.astype(jnp.int32))
        source = jnp.max(jnp.where(hit, page_id, 0)) // page_count
        source = lax.rem(source, tp_count)
        cache[s] = jnp.where(found > 0, incoming[source], jnp.zeros_like(incoming[0]))
    for group in (core_copies, y_copies, w_copies, z_copies, page_copies):
        for copy in group.values():
            copy.wait_send()
    for copy in ag_copies + [c for pair in last_copies for c in pair]:
        copy.wait_send()


def on_device(
    hidden_states, w_query, w_key_value, kv_pages, row_pages, last_pad, page_dest, page_slot
):
    steps, row_count, width_part = hidden_states.shape
    n = lax.axis_size(("pool", "tp"))
    tp_count = lax.axis_size("tp")
    z_count = tp_count // 2
    slot_count = tp_count // 2
    rows = steps * row_count
    flat_rows = hidden_states.reshape(rows, width_part)
    positions = (row_pages * PAGE - last_pad)[None, :] + jnp.arange(steps, dtype=jnp.int32)[:, None]
    half_size = HD // 2
    frequency = 500000.0 ** (-jnp.arange(half_size, dtype=jnp.float32) * 2.0 / HD)
    frequency = jnp.concatenate([frequency, frequency])
    angles = positions.astype(jnp.float32).reshape(rows, 1) * frequency
    cosine = jnp.cos(angles)
    sine = jnp.sin(angles) * jnp.where(jnp.arange(HD) < half_size, -1.0, 1.0)
    page_count, page_len, page_width = kv_pages.shape

    heads = QH // n
    cols = heads * HD
    owners = n // KVH
    lanes = heads * page_count * steps
    index = np.arange(n * lanes).reshape(n, heads, page_count, steps)
    source, head, page, step = np.unravel_index(index, index.shape)
    src_page = (source * page_count + page).astype(np.int32).reshape(n, lanes)
    src_base = (head * rows + step * row_count).astype(np.int32).reshape(n, lanes)
    row_page = page[:owners].astype(np.int32).reshape(owners * lanes, 1)

    vmem = pl.BlockSpec(memory_space=pltpu.VMEM)
    smem = pl.BlockSpec(memory_space=pltpu.SMEM)
    hbm = pl.BlockSpec(memory_space=pl.ANY)
    dma = pltpu.SemaphoreType.DMA
    block = (rows, cols + 2 * HD)
    f32, bf16 = jnp.float32, jnp.bfloat16
    attn, decode_cache = pl.pallas_call(
        functools.partial(kernel, n, tp_count, steps, slot_count),
        out_shape=(
            jax.ShapeDtypeStruct((rows, cols), bf16),
            jax.ShapeDtypeStruct((slot_count, page_len, page_width), bf16),
        ),
        in_specs=[smem, smem, vmem, hbm, hbm] + [vmem] * 10,
        out_specs=(vmem, vmem),
        scratch_shapes=[
            pltpu.VMEM((n, width_part, cols), bf16),
            pltpu.VMEM(w_key_value.shape, bf16),
            pltpu.VMEM((rows, w_key_value.shape[1]), f32),
            pltpu.VMEM((z_count, 2) + block, f32),
            pltpu.VMEM((z_count, 2) + block, f32),
            pltpu.VMEM((z_count,) + block, f32),
            pltpu.VMEM((z_count,) + block, f32),
            pltpu.VMEM((z_count,) + block, f32),
            pltpu.VMEM((z_count // 2,) + block, f32),
            pltpu.VMEM((z_count // 2,) + block, f32),
            pltpu.VMEM((z_count // 2,) + block, jnp.float32),
            pltpu.VMEM((z_count // 2,) + block, jnp.float32),
            pltpu.VMEM((heads * rows, HD), bf16),
            pltpu.VMEM((n, lanes, HD), bf16),
            pltpu.VMEM((n, lanes, HD), bf16),
            pltpu.VMEM((n, lanes, HD), jnp.bfloat16),
            pltpu.VMEM((n, lanes, HD), jnp.bfloat16),
            pltpu.VMEM((n, 8, lanes), f32),
            pltpu.VMEM((n, 8, lanes), f32),
            pltpu.VMEM((n, lanes), jnp.int32),
            pltpu.VMEM((tp_count, page_len, page_width), bf16),
            pltpu.VMEM((tp_count, page_len, page_width), bf16),
            dma((n + 1,)),
            dma((tp_count,)),
            dma((tp_count,)),
            dma((z_count, 2)),
            dma((z_count, 2)),
        ]
        + [dma((z_count,))] * 2
        + [dma((z_count // 2,))] * 4
        + [dma((n,))] * 6,
        compiler_params=pltpu.CompilerParams(
            collective_id=0, has_side_effects=True, vmem_limit_bytes=62 * 1024 * 1024
        ),
    )(
        row_pages, last_pad, flat_rows, w_query, w_key_value, kv_pages,
        page_dest.reshape(1, -1), page_slot.reshape(1, -1), cosine, sine,
        src_page.reshape(1, -1), src_base.reshape(1, -1), src_page, src_base, row_page,
    )
    return (attn.reshape(steps, row_count, cols), decode_cache)


def solution(mesh):
    placed = (
        P(None, "groups", ("pool", "tp")),
        P(("pool", "tp"), None),
        P(("pool", "tp"), None),
        P(("groups", "pool", "tp"), None, None),
        P("groups"),
        P("groups"),
        P("groups"),
        P("groups"),
    )
    return jax.shard_map(
        on_device,
        mesh=mesh,
        in_specs=placed,
        out_specs=(P(None, "groups", ("pool", "tp")), P(("groups", "pool", "tp"), None, None)),
        check_vma=False,
    )
```
